256 devices in a mesh: dp: 32 (over y, x, z_lo), layer: 8 (over z_hi, core).
Axes of the slice: x: 4, y: 4, z: 8 (z_hi: 4, z_lo: 2; z = z_hi * 2 + z_lo), core: 2. Of those that a mesh axis runs over, the one named last changes fastest.
Arguments:
- layer_inputs: bfloat16 [8, 32768, 4096], P('layer', 'dp'), may hold values from -6 to 6
- output_grads: bfloat16 [8, 32768, 512], P('layer', 'dp'), may hold values from -6 to 6
- input_factors: bfloat16 [256, 8, 4, 4096], P('dp', 'layer'), may hold values from -0.09375 to 0.09375
- output_factors: bfloat16 [256, 8, 4, 512], P('dp', 'layer'), may hold values from -0.25 to 0.25
Outputs:
- scores: float32 [256, 32768], P(None, 'dp')
The draws below stay inside these ranges and needn't reach their ends.
All inputs are finite; a program needn't handle non-finite values.
Results may differ from the reference program's by a relative error of at most 0.0003.
Values may be sent and summed in bfloat16 or wider, within the bound.
No kernel may reach another device: no remote copies, remote signals or barrier semaphores. Data moves between devices by JAX's collectives and lax.ppermute only.
A program may use at most 128 MiB of HBM per device.

```python
import jax
import jax.numpy as jnp
from jax import lax

D = 4096
KV = 512
RANK = 4
LAYERS = 8
TOKENS = 32768
QUERIES = 256


def shard_levels(key, extent, shards, least, high):
    gain = 1.0
    for dim, blocks in shards:
        steps = jax.random.uniform(jax.random.fold_in(jax.random.fold_in(key, 6), dim), (blocks,), jnp.float32, least / len(shards), high / len(shards))
        gain = gain * jnp.repeat(jnp.exp(steps), extent[dim] // blocks).reshape((-1,) + (1,) * (len(extent) - 1 - dim))
    return gain


def gaussian(rng, dims, deviation, most, shards=(), held_as=jnp.bfloat16):
    entries = jax.random.normal(rng, dims, jnp.float32) * deviation
    if len(shards) > 0:
        entries = shard_levels(rng, dims, shards, -0.22, 0.18) * entries
    return jnp.clip(entries, min=-most, max=most).astype(held_as)


def setup_inputs(seed: int = 0) -> dict:
    key_of = jax.random.split(jax.random.key(seed), 5)
    return {
        "layer_inputs": gaussian(key_of[0], (LAYERS, TOKENS, D), 1.0, 6.0, ((0, 8), (1, 32))),
        "output_grads": gaussian(key_of[1], (LAYERS, TOKENS, KV), 1.0, 6.0, ((0, 8), (1, 32))),
        "input_factors": gaussian(key_of[2], (QUERIES, LAYERS, RANK, D), D ** -0.5, 0.09375, ((0, 32), (1, 8))),
        "output_factors": gaussian(key_of[3], (QUERIES, LAYERS, RANK, KV), KV ** -0.5, 0.25, ((0, 32), (1, 8))),
    }


def layer_term(acts, grads, in_fac, out_fac):
    count = in_fac.shape[0]
    in_flat = in_fac.reshape(count * in_fac.shape[1], in_fac.shape[2])
    out_flat = out_fac.reshape(count * out_fac.shape[1], out_fac.shape[2])
    proj_in = lax.dot_general(acts, in_flat, (((1,), (1,)), ((), ())), preferred_element_type=jnp.float32)
    proj_out = lax.dot_general(grads, out_flat, (((1,), (1,)), ((), ())), preferred_element_type=jnp.float32)
    joined = (proj_in * proj_out).reshape(acts.shape[0], count, in_fac.shape[1])
    return jnp.sum(joined, axis=2).T


def reference(layer_inputs, output_grads, input_factors, output_factors):
    in_layers = jnp.moveaxis(input_factors, 1, 0)
    out_layers = jnp.moveaxis(output_factors, 1, 0)

    def step(total, items):
        acts, grads, in_fac, out_fac = items
        return total + layer_term(acts, grads, in_fac, out_fac), None

    start = jnp.zeros((QUERIES, TOKENS), jnp.float32)
    total, unused = lax.scan(step, start, (layer_inputs, output_grads, in_layers, out_layers))
    return total
```

```python
import functools

import jax
import jax.numpy as jnp
from jax import lax
from jax.experimental import pallas as pl
from jax.experimental.pallas import tpu as pltpu
from jax.sharding import PartitionSpec as P

NY, NX, NZ = 4, 4, 2
RANK = 4
QPD = 8
ROWS = RANK * QPD
HALF = ROWS // 2
TB = 256


def dp_of(y, x, z):
    return ((y % NY) * NX + x % NX) * NZ + z % NZ


def dp_perm(dy, dx, dz):
    return [
        (dp_of(y, x, z), dp_of(y + dy, x + dx, z + dz))
        for y in range(NY)
        for x in range(NX)
        for z in range(NZ)
    ]


STEPS = {
    "XP": dp_perm(0, 1, 0),
    "XM": dp_perm(0, -1, 0),
    "YP": dp_perm(1, 0, 0),
    "YM": dp_perm(-1, 0, 0),
    "Z": dp_perm(0, 0, 1),
}
MOVE = {"XP": (0, -1, 0), "XM": (0, 1, 0), "YP": (0, 0, -1), "YM": (0, 0, 1), "Z": (1, 0, 0)}
CORE_SWAP = [(i, i ^ 1) for i in range(8)]


def layer_pairs(first):
    out = []
    for zh in range(4):
        for core in range(2):
            even = core == first
            other = zh ^ 1 if even else ((zh + 1) % 4 if zh % 2 == 1 else (zh - 1) % 4)
            out.append((zh * 2 + core, other * 2 + core))
    return out


PAIR_A, PAIR_B = layer_pairs(0), layer_pairs(1)


def wrap(d):
    return (d + 1) % 4 - 1


def moved(piece, step):
    plane, dx, dy, part = piece
    mz, mx, my = MOVE[step]
    return (plane ^ mz, wrap(dx + mx), wrap(dy + my), part)


def piece_rows(piece):
    return ROWS if piece[3] is None else HALF


class Pieces:
    def __init__(self, own):
        self.where = {(0, 0, 0, None): (own, 0)}

    def get(self, piece):
        if piece in self.where:
            buf, at = self.where[piece]
            n = piece_rows(piece)
            return buf if buf.shape[0] == n else lax.slice_in_dim(buf, at, at + n, axis=0)
        whole = piece[:3] + (None,)
        if whole in self.where:
            buf, at = self.where[whole]
            at += piece[3] * HALF
            return lax.slice_in_dim(buf, at, at + HALF, axis=0)
        return jnp.concatenate([self.get(piece[:3] + (h,)) for h in (0, 1)], axis=0)

    def send(self, step, pieces):
        parts = [self.get(p) for p in pieces]
        data = parts[0] if len(parts) == 1 else jnp.concatenate(parts, axis=0)
        got = lax.ppermute(data, "dp", STEPS[step])
        at, names = 0, []
        for p in pieces:
            q = moved(p, step)
            self.where[q] = (got, at)
            names.append(q)
            at += piece_rows(q)
        return got, names


def term_kernel(n_buf, plan, blocks, x_ref, g_ref, *refs):
    bufs, out_ref, fac = refs[:n_buf], refs[n_buf], refs[n_buf + 1]
    core = lax.rem(lax.axis_index("layer"), 2)
    at = 0
    for b in bufs:
        fac[at : at + b.shape[0], :] = b[...]
        at += b.shape[0]
    depth = x_ref.shape[1]
    half = len(blocks) // 2

    @pl.loop(0, x_ref.shape[0] // TB)
    def _(i):
        t = pl.multiple_of(i * TB, TB)
        dims = (((1,), (1,)), ((), ()))
        a = lax.dot_general(
            fac[:, :depth], x_ref[pl.ds(t, TB), :], dims, preferred_element_type=jnp.float32
        )
        b = lax.dot_general(
            fac[:, depth:], g_ref[pl.ds(t, TB), :], dims, preferred_element_type=jnp.float32
        )
        c = a * b
        for k, block in enumerate(blocks):
            tiles = [c[r : r + QPD, :] for r in plan[block]]
            total = (tiles[0] + tiles[1]) + (tiles[2] + tiles[3])
            h, row = divmod(k, half)
            which = jnp.bitwise_xor(core, h)
            out_ref[which, row * QPD : (row + 1) * QPD, pl.ds(t, TB)] = total


def term(x, g, received):
    plan, at = {}, 0
    for _, names in received:
        for name in names:
            n = piece_rows(name)
            plan.setdefault(name[:3], []).extend(range(at, at + n, QPD))
            at += n
    blocks = sorted(plan)
    assert all(len(v) == RANK for v in plan.values()) and len(blocks) % 2 == 0
    vmem = pl.BlockSpec(memory_space=pltpu.VMEM)
    tokens, width = x.shape[0], x.shape[1] + g.shape[1]
    out = pl.pallas_call(
        functools.partial(term_kernel, len(received), plan, blocks),
        out_shape=jax.ShapeDtypeStruct((2, len(blocks) // 2 * QPD, tokens), jnp.float32),
        in_specs=[vmem] * (2 + len(received)),
        out_specs=vmem,
        scratch_shapes=[pltpu.VMEM((at, width), jnp.bfloat16)],
        compiler_params=pltpu.CompilerParams(vmem_limit_bytes=20 * 2**20),
        cost_estimate=pl.CostEstimate(
            flops=2 * at * width * tokens, bytes_accessed=at * width * 2, transcendentals=0
        ),
    )(x, g, *[b for b, _ in received])
    return out, blocks


def layer_sum(terms):
    keep = [t[0] for t in terms]
    send = [t[1] for t in terms]
    keep = keep[0] if len(keep) == 1 else jnp.concatenate(keep, axis=0)
    send = send[0] if len(send) == 1 else jnp.concatenate(send, axis=0)
    mine = keep + lax.ppermute(send, "layer", CORE_SWAP)
    mine = mine + lax.ppermute(mine, "layer", PAIR_A)
    mine = mine + lax.ppermute(mine, "layer", PAIR_B)
    return mine, lax.ppermute(mine, "layer", CORE_SWAP)


def place_kernel(groups, *refs):
    out_ref = refs[-1]
    core = lax.rem(lax.axis_index("layer"), 2)
    d = lax.axis_index("dp")
    z, x, y = lax.rem(d, NZ), lax.rem(d // NZ, NX), d // (NZ * NX)
    for g, halves in enumerate(groups):
        for h in range(2):
            for row, (plane, dx, dy) in enumerate(halves[h]):
                at = ((lax.rem(y + dy + NY, NY) * NX + lax.rem(x + dx + NX, NX)) * NZ
                      + jnp.bitwise_xor(z, plane)) * QPD
                rows = pl.ds(row * QPD, QPD)
                mine, other = refs[2 * g], refs[2 * g + 1]

                @pl.when(core == h)
                def _():
                    out_ref[pl.ds(pl.multiple_of(at, QPD), QPD), :] = mine[rows, :]

                @pl.when(core != h)
                def _():
                    out_ref[pl.ds(pl.multiple_of(at, QPD), QPD), :] = other[rows, :]


def place(groups, arrays, queries):
    vmem = pl.BlockSpec(memory_space=pltpu.VMEM)
    return pl.pallas_call(
        functools.partial(place_kernel, groups),
        out_shape=jax.ShapeDtypeStruct((queries, arrays[0].shape[1]), jnp.float32),
        in_specs=[vmem] * len(arrays),
        out_specs=vmem,
        compiler_params=pltpu.CompilerParams(vmem_limit_bytes=12 * 2**20),
    )(*arrays)


def shards(layer_inputs, output_grads, input_factors, output_factors):
    x, g = layer_inputs[0], output_grads[0]
    own = jnp.concatenate([input_factors[:, 0], output_factors[:, 0]], axis=2)
    own = jnp.swapaxes(own, 0, 1).reshape(ROWS, own.shape[2])
    have = Pieces(own)
    A, B = 0, 1
    rz = have.send("Z", [(A, 0, 0, None)])
    first = [have.send(s, [(A, 0, 0, None)]) for s in ("XP", "XM", "YP", "YM")]
    c0 = [(own, [(A, 0, 0, None)]), rz] + first
    c1 = [
        have.send("XP", [(A, -1, 0, 1), (B, 0, 0, None)]),
        have.send("XM", [(A, 1, 0, 0), (B, 0, 0, None)]),
        have.send("YP", [(A, 0, -1, 1), (B, 0, 0, None)]),
        have.send("YM", [(A, 0, 1, 0), (B, 0, 0, None)]),
    ]
    c2 = [have.send(s, [(A, 1, 0, None), (A, -1, 0, None)]) for s in ("YP", "YM")]
    c3 = [
        have.send("XP", [(B, -1, 0, 1), (B, 0, 1, None), (B, 0, -1, None)]),
        have.send("XM", [(B, 1, 0, 0), (B, 0, 1, None), (B, 0, -1, None)]),
        have.send("YP", [(B, 0, -1, 1), (A, 2, 0, None)]),
        have.send("YM", [(B, 0, 1, 0), (A, 2, 0, None)]),
    ]
    c4 = [
        have.send("XP", [(B, -1, 1, 1), (B, -1, -1, 1)]),
        have.send("XM", [(B, 1, 1, 0), (B, 1, -1, 0)]),
        have.send("YP", [(A, 1, -1, 1), (A, -1, -1, 1)]),
        have.send("YM", [(A, 1, 1, 0), (A, -1, 1, 0)]),
        have.send("XP", [(B, 0, 2, None)]),
        have.send("XM", [(B, 0, 2, None)]),
    ]
    c5 = [
        have.send("YP", [(A, 2, -1, 1)]),
        have.send("YM", [(A, 2, 1, 0)]),
        have.send("XP", [(B, -1, 2, 1)]),
        have.send("XM", [(B, 1, 2, 0)]),
    ]
    groups, arrays = [], []
    for chunks in ((c0, c1), (c2, c3), (c4, c5)):
        terms, halves = [], ([], [])
        for c in chunks:
            out, blocks = term(x, g, c)
            terms.append(out)
            halves[0].extend(blocks[: len(blocks) // 2])
            halves[1].extend(blocks[len(blocks) // 2 :])
        arrays.extend(layer_sum(terms))
        groups.append(halves)
    return place(groups, arrays, lax.axis_size("dp") * QPD)


def solution(mesh):
    in_specs = (
        P("layer", "dp", None),
        P("layer", "dp", None),
        P("dp", "layer", None, None),
        P("dp", "layer", None, None),
    )
    out_specs = P(None, "dp")
    return jax.shard_map(shards, mesh=mesh, in_specs=in_specs, out_specs=out_specs, check_vma=False)
```

```python
import functools

import jax
import jax.numpy as jnp
from jax import lax
from jax.experimental import pallas as pl
from jax.experimental.pallas import tpu as pltpu
from jax.sharding import PartitionSpec as P

NY, NX, NZ = 4, 4, 2
RANK = 4
QPD = 8
ROWS = RANK * QPD
HALF = ROWS // 2
TB = 256


def dp_of(y, x, z):
    return ((y % NY) * NX + x % NX) * NZ + z % NZ


def dp_perm(dy, dx, dz):
    return [
        (dp_of(y, x, z), dp_of(y + dy, x + dx, z + dz))
        for y in range(NY)
        for x in range(NX)
        for z in range(NZ)
    ]


STEPS = {
    "XP": dp_perm(0, 1, 0),
    "XM": dp_perm(0, -1, 0),
    "YP": dp_perm(1, 0, 0),
    "YM": dp_perm(-1, 0, 0),
    "Z": dp_perm(0, 0, 1),
}
MOVE = {"XP": (0, -1, 0), "XM": (0, 1, 0), "YP": (0, 0, -1), "YM": (0, 0, 1), "Z": (1, 0, 0)}
CORE_SWAP = [(i, i ^ 1) for i in range(8)]


def layer_pairs(first):
    out = []
    for zh in range(4):
        for core in range(2):
            even = core == first
            other = zh ^ 1 if even else ((zh + 1) % 4 if zh % 2 == 1 else (zh - 1) % 4)
            out.append((zh * 2 + core, other * 2 + core))
    return out


PAIR_A, PAIR_B = layer_pairs(0), layer_pairs(1)


def wrap(d):
    return (d + 1) % 4 - 1


def moved(piece, step):
    plane, dx, dy, part = piece
    mz, mx, my = MOVE[step]
    return (plane ^ mz, wrap(dx + mx), wrap(dy + my), part)


def piece_rows(piece):
    return ROWS if piece[3] is None else HALF


class Pieces:
    def __init__(self, own):
        self.where = {(0, 0, 0, None): (own, 0)}

    def get(self, piece):
        if piece in self.where:
            buf, at = self.where[piece]
            n = piece_rows(piece)
            return buf if buf.shape[0] == n else lax.slice_in_dim(buf, at, at + n, axis=0)
        whole = piece[:3] + (None,)
        if whole in self.where:
            buf, at = self.where[whole]
            at += piece[3] * HALF
            return lax.slice_in_dim(buf, at, at + HALF, axis=0)
        return jnp.concatenate([self.get(piece[:3] + (h,)) for h in (0, 1)], axis=0)

    def pack(self, pieces, *behind):
        parts = [self.get(p) for p in pieces]
        data = parts[0] if len(parts) == 1 else jnp.concatenate(parts, axis=0)
        return (after(data, *behind) if behind else data), pieces

    def send(self, step, packed):
        data, pieces = packed
        got = lax.ppermute(data, "dp", STEPS[step])
        at, names = 0, []
        for p in pieces:
            q = moved(p, step)
            self.where[q] = (got, at)
            names.append(q)
            at += piece_rows(q)
        return got, names


def after(value, *others):
    return lax.optimization_barrier((value,) + others)[0]


def term_kernel(segments, plan, blocks, x_ref, g_ref, *refs):
    bufs, out_ref, fac = refs[: len(segments)], refs[-2], refs[-1]
    core = lax.rem(lax.axis_index("layer"), 2)
    at = 0
    for b, parts in zip(bufs, segments):
        for begin, n in parts:
            fac[at : at + n, :] = b[begin : begin + n, :]
            at += n
    depth = x_ref.shape[1]
    half = len(blocks) // 2

    @pl.loop(0, x_ref.shape[0] // TB)
    def _(i):
        t = pl.multiple_of(i * TB, TB)
        dims = (((1,), (1,)), ((), ()))
        a = lax.dot_general(
            fac[:, :depth], x_ref[pl.ds(t, TB), :], dims, preferred_element_type=jnp.float32
        )
        b = lax.dot_general(
            fac[:, depth:], g_ref[pl.ds(t, TB), :], dims, preferred_element_type=jnp.float32
        )
        c = a * b
        for k, block in enumerate(blocks):
            tiles = [c[r : r + QPD, :] for r in plan[block]]
            total = (tiles[0] + tiles[1]) + (tiles[2] + tiles[3])
            h, row = divmod(k, half)
            which = jnp.bitwise_xor(core, h)
            out_ref[which, row * QPD : (row + 1) * QPD, pl.ds(t, TB)] = total


def term(x, g, received, leave=()):
    plan, segments, at = {}, [], 0
    for _, names in received:
        parts, row = [], 0
        for name in names:
            n = piece_rows(name)
            if name[:3] not in leave:
                parts.append((row, n))
                plan.setdefault(name[:3], []).extend(range(at, at + n, QPD))
                at += n
            row += n
        segments.append(parts)
    blocks = sorted(plan)
    assert all(len(v) == RANK for v in plan.values()) and len(blocks) % 2 == 0
    vmem = pl.BlockSpec(memory_space=pltpu.VMEM)
    tokens, width = x.shape[0], x.shape[1] + g.shape[1]
    out = pl.pallas_call(
        functools.partial(term_kernel, segments, plan, blocks),
        out_shape=jax.ShapeDtypeStruct((2, len(blocks) // 2 * QPD, tokens), jnp.float32),
        in_specs=[vmem] * (2 + len(received)),
        out_specs=vmem,
        scratch_shapes=[pltpu.VMEM((at, width), jnp.bfloat16)],
        compiler_params=pltpu.CompilerParams(vmem_limit_bytes=20 * 2**20),
        cost_estimate=pl.CostEstimate(flops=1 * 2 * at * width * tokens, bytes_accessed=1, transcendentals=0),
    )(x, g, *[b for b, _ in received])
    return out, blocks


def to_core(terms, h):
    parts = [t[h] for t in terms]
    return parts[0] if len(parts) == 1 else jnp.concatenate(parts, axis=0)


def layer_move(value, pairs):
    return lax.ppermute(value, "layer", pairs)


def place_kernel(groups, *refs):
    out_ref = refs[-1]
    core = lax.rem(lax.axis_index("layer"), 2)
    d = lax.axis_index("dp")
    z, x, y = lax.rem(d, NZ), lax.rem(d // NZ, NX), d // (NZ * NX)
    for g, halves in enumerate(groups):
        for h in range(2):
            for row, (plane, dx, dy) in enumerate(halves[h]):
                at = ((lax.rem(y + dy + NY, NY) * NX + lax.rem(x + dx + NX, NX)) * NZ
                      + jnp.bitwise_xor(z, plane)) * QPD
                rows = pl.ds(row * QPD, QPD)
                mine, other = refs[2 * g], refs[2 * g + 1]

                @pl.when(core == h)
                def _():
                    out_ref[pl.ds(pl.multiple_of(at, QPD), QPD), :] = mine[rows, :]

                @pl.when(core != h)
                def _():
                    out_ref[pl.ds(pl.multiple_of(at, QPD), QPD), :] = other[rows, :]


def place(groups, arrays, queries):
    vmem = pl.BlockSpec(memory_space=pltpu.VMEM)
    return pl.pallas_call(
        functools.partial(place_kernel, groups),
        out_shape=jax.ShapeDtypeStruct((queries, arrays[0].shape[1]), jnp.float32),
        in_specs=[vmem] * len(arrays),
        out_specs=vmem,
        compiler_params=pltpu.CompilerParams(vmem_limit_bytes=12 * 2**20),
    )(*arrays)


def shards(layer_inputs, output_grads, input_factors, output_factors):
    acts, grads = layer_inputs[0], output_grads[0]
    own = jnp.concatenate([input_factors[:, 0], output_factors[:, 0]], axis=2)
    own = jnp.swapaxes(own, 0, 1).reshape(ROWS, own.shape[2])
    have = Pieces(own)
    A, B = 0, 1
    B0 = (B, 0, 0, None)
    mine = (own, [(A, 0, 0, None)])
    z0 = have.send("Z", mine)
    xy0 = [have.send(s, mine) for s in ("XP", "XM", "YP", "YM")]

    x = [have.pack([(A, -1, 0, 1), B0]), have.pack([(A, 1, 0, 0), B0])]
    y = [have.pack([(A, 0, -1, 1), B0]), have.pack([(A, 0, 1, 0), B0])]
    x1 = [have.send("XP", x[0]), have.send("XM", x[1])]
    y1 = [have.send("YP", y[0]), have.send("YM", y[1])]

    y = [have.pack([(B, 0, -1, 1), (A, 2, 0, None)]), have.pack([(B, 0, 1, 0), (A, 2, 0, None)])]
    x = [
        have.pack([(B, -1, 0, 1), (B, 0, 1, None), (B, 0, -1, None)]),
        have.pack([(B, 1, 0, 0), (B, 0, 1, None), (B, 0, -1, None)]),
    ]
    y2 = [have.send("YP", y[0]), have.send("YM", y[1])]
    x2 = [have.send("XP", x[0]), have.send("XM", x[1])]

    t0, blocks0 = term(acts, grads, [(after(z0[0], x[0][0], x[1][0], y[0][0], y[1][0]), z0[1])] + xy0 + x1)

    r0 = layer_move(to_core((t0,), 1), CORE_SWAP)

    y = have.pack([(A, 1, 0, None), (A, -1, 0, None)], t0)
    y3 = [have.send("YP", y), have.send("YM", y)]

    x = [
        have.pack([(B, 0, 2, None), (B, -1, 1, 1), (B, -1, -1, 1)], y3[0][0], y3[1][0]),
        have.pack([(B, 0, 2, None), (B, 1, 1, 0), (B, 1, -1, 0)], y3[0][0], y3[1][0]),
    ]
    y = [
        have.pack([(A, 1, -1, 1), (A, -1, -1, 1), (A, 2, -1, 1)], x2[0][0], x2[1][0]),
        have.pack([(A, 1, 1, 0), (A, -1, 1, 0), (A, 2, 1, 0)], x2[0][0], x2[1][0]),
    ]
    x3 = [have.send("XP", x[0]), have.send("XM", x[1])]
    y4 = [have.send("YP", y[0]), have.send("YM", y[1])]

    s0 = to_core((t0,), 0) + after(r0, x[0][0], x[1][0], y[0][0], y[1][0])
    r0 = layer_move(s0, PAIR_A)
    late = {(B, i, j) for i in (-1, 1) for j in (-1, 1)}
    t1, blocks1 = term(acts, grads, [(after(own, s0), mine[1])] + y1 + y2 + x2, late)
    s0 = s0 + after(r0, t1)
    r0 = layer_move(s0, PAIR_B)
    t2, blocks2 = term(acts, grads, x2 + [(after(b, s0), n) for b, n in y3], {(B, 2, 0)})
    r1 = layer_move(to_core((t1, t2), 1), CORE_SWAP)
    s0 = s0 + after(r0, t2)

    x = [have.pack([(B, -1, 2, 1)], t2), have.pack([(B, 1, 2, 0)], t2)]
    x4 = [have.send("XP", x[0]), have.send("XM", x[1])]
    s1 = to_core((t1, t2), 0) + after(r1, x[0][0], x[1][0])
    r1 = layer_move(s1, PAIR_A)

    t3, blocks3 = term(acts, grads, x3 + [(after(b, s1), n) for b, n in y4] + x4)
    r2 = layer_move(to_core((t3,), 1), CORE_SWAP)
    s1 = s1 + after(r1, t3)
    r1 = layer_move(s1, PAIR_B)
    s2 = to_core((t3,), 0) + after(r2, s1)
    r2 = layer_move(s2, PAIR_A)
    o0 = layer_move(s0, CORE_SWAP)
    s1 = s1 + after(r1, s2)
    o1 = layer_move(s1, CORE_SWAP)
    s2 = s2 + after(r2, s1)
    s2 = s2 + layer_move(s2, PAIR_B)
    o2 = layer_move(s2, CORE_SWAP)

    def halves(*blocks):
        return [sum((b[: len(b) // 2] for b in blocks), []), sum((b[len(b) // 2 :] for b in blocks), [])]

    groups = [halves(blocks0), halves(blocks1, blocks2), halves(blocks3)]
    return place(groups, [s0, o0, s1, o1, s2, o2], lax.axis_size("dp") * QPD)


def solution(mesh):
    in_specs = (
        P("layer", "dp", None),
        P("layer", "dp", None),
        P("dp", "layer", None, None),
        P("dp", "layer", None, None),
    )
    out_specs = P(None, "dp")
    return jax.shard_map(shards, mesh=mesh, in_specs=in_specs, out_specs=out_specs, check_vma=False)
```
